256 devices in a mesh: aux: 32 (over z, x_lo, core), row: 8 (over y, x_hi).
Axes of the slice: x: 4 (x_hi: 2, x_lo: 2; x = x_hi * 2 + x_lo), y: 4, z: 8, core: 2. Of those that a mesh axis runs over, the one named last changes fastest.
Arguments:
- three_center: bfloat16 [1536, 8, 64, 512], P('aux', 'row'), may hold values from -2 to 2
- coefficients: bfloat16 [1024, 10240], P('aux'), may hold values from -6 to 6
- col_tiles: int32 [8, 8], P('row'), may hold values from 0 to 159, as said below
- tile_count: int32 [8], P('row'), may hold values from 1 to 8, as said below
Outputs:
- exchange_tiles: float32 [512, 512], P('row', 'aux')
- exchange_diagonal: float32 [512], P('row')
The draws below stay inside these ranges and needn't reach their ends.
Inputs may be any that keep to these rules, and one draw needn't show every extreme that they name: `col_tiles`: the slots of one row tile name different column tiles. `tile_count`: some row tile has all 8 slots live.
All inputs are finite; a program needn't handle non-finite values.
Results may differ from the reference program's by a relative error of at most 0.0034.
Values may be sent and summed in bfloat16 or wider, within the bound.
No kernel may reach another device: no remote copies, remote signals or barrier semaphores. Data moves between devices by JAX's collectives and lax.ppermute only.
A program may use at most 128 MiB of HBM per device.

```python
import jax
import jax.numpy as jnp
from jax import lax

NBF = 10240
NOCC = 1024
TB = 64
NZMAX = 8
AUXD = 48
AUX = 1536
NROWT = 8


def draw_three_center(key, part):
    key = jax.random.fold_in(key, 5)
    key_main = jax.random.fold_in(key, 0)
    shape = (AUX, NROWT, TB, NZMAX * TB)
    position = jnp.arange(AUX, dtype=jnp.float32) / jnp.float32(max(AUX - 1, 1))
    values = jax.random.normal(key_main, shape, jnp.float32)
    amplitude = jnp.exp(0.5 * jnp.log(3.0) * position)
    scaled = values * amplitude[:, None, None, None] / jnp.sqrt(jnp.float32(NZMAX * TB))
    return jnp.clip(scaled, -2.0, 2.0).astype(jnp.bfloat16)


def draw_col_tiles(key, part):
    key = jax.random.fold_in(key, 11)
    ntiles = NBF // TB
    key_base, key_step = jax.random.split(key)
    base = jax.random.randint(key_base, (NROWT, 1), 0, ntiles)
    stride = jax.random.randint(key_step, (NROWT, 1), 1, ntiles // NZMAX + 1)
    slots = jnp.arange(NZMAX, dtype=jnp.int32)[None, :]
    return ((base + slots * stride) % ntiles).astype(jnp.int32)


def draw_tile_count(key, part):
    key = jax.random.fold_in(key, 23)
    key_count, key_full = jax.random.split(key)
    counts = jax.random.randint(key_count, (NROWT,), 1, NZMAX + 1)
    full = jax.random.randint(key_full, (), 0, NROWT)
    rows = jnp.arange(NROWT, dtype=jnp.int32)
    return jnp.where(rows == full, NZMAX, counts).astype(jnp.int32)


def block_scale(key, extent, cuts, low, largest):
    factor_of, own = 1.0, jax.random.fold_in(key, 6)
    for dim, parts in cuts:
        heights = jnp.exp(jax.random.uniform(jax.random.fold_in(own, dim), (parts,), jnp.float32, low / len(cuts), largest / len(cuts)))
        factor_of = factor_of * jnp.repeat(heights, extent[dim] // parts).reshape([-1 if axis == dim else 1 for axis in range(len(extent))])
    return factor_of


def scatter_about(stream_key, shape, spread, most, shards=(), kind=jnp.bfloat16):
    entries = spread * jax.random.normal(stream_key, shape, jnp.float32)
    if shards:
        entries = entries * block_scale(stream_key, shape, shards, -0.22, 0.18)
    return jnp.clip(entries, -most, most).astype(kind)


def setup_inputs(seed: int = 0) -> dict:
    keys = jax.random.split(jax.random.key(seed), 5)
    three_center = draw_three_center(jax.random.fold_in(keys[4], 71), 0)
    coefficients = scatter_about(keys[1], (NOCC, NBF), 1.0, 6.0, ((0, 32),))
    col_tiles = draw_col_tiles(jax.random.fold_in(keys[4], 71), 0)
    tile_count = draw_tile_count(jax.random.fold_in(keys[4], 71), 0)
    return {"three_center": three_center, "coefficients": coefficients, "col_tiles": col_tiles, "tile_count": tile_count}


def reference(three_center, coefficients, col_tiles, tile_count):
    ntiles = NBF // TB
    slots = jnp.arange(NZMAX, dtype=jnp.int32)
    active_tiles = slots[None, :] < tile_count[:, None]
    ctiles = coefficients.reshape(NOCC, ntiles, TB)
    chosen_tiles = jnp.take(ctiles, col_tiles.reshape(-1).astype(jnp.int32), axis=1).reshape(NOCC, NROWT, NZMAX, TB)
    chosen_tiles = jnp.where(active_tiles[None, :, :, None], chosen_tiles, jnp.zeros((), jnp.bfloat16)).reshape(NOCC, NROWT, NZMAX * TB)
    picked32 = chosen_tiles.astype(jnp.float32)
    blocks = three_center.reshape(AUX // AUXD, AUXD, NROWT, TB, NZMAX * TB)

    def step(carry, block):
        total, diagonal = carry
        half = jnp.einsum('qrmk,irk->qrmi', block.astype(jnp.float32), picked32)
        half = half.astype(jnp.bfloat16).astype(jnp.float32).reshape(AUXD, NROWT * TB, NOCC)
        total = total + jnp.einsum('qmi,qni->mn', half, half)
        diagonal = diagonal + lax.optimization_barrier(jnp.sum(half * half, axis=(0, 2)))
        return ((total, diagonal), None)
    start = (jnp.zeros((NROWT * TB, NROWT * TB), jnp.float32), jnp.zeros((NROWT * TB,), jnp.float32))
    (total, diagonal), _ = lax.scan(step, start, blocks)
    positions = jnp.arange(NROWT * TB, dtype=jnp.int32)
    on_diagonal = positions[:, None] == positions[None, :]
    total = jnp.where(on_diagonal, jnp.zeros((), jnp.float32), total)
    exchange_tiles = total / jnp.sqrt(jnp.float32(AUX * NOCC))
    exchange_diagonal = diagonal / jnp.float32(AUX * NOCC)
    return (exchange_tiles, exchange_diagonal)
```

```python
import functools

import jax
import jax.numpy as jnp
from jax import lax
from jax.experimental import pallas as pl
from jax.experimental.pallas import tpu as pltpu
from jax.sharding import Mesh, PartitionSpec as P

ROW = ("y", "xh")
AUX = ("z", "xl", "c")


def pick_kernel(copies, width, col_ref, count_ref, coef_ref, out_ref):
    slots = col_ref.shape[0]
    for pair in range(slots // 2):
        halves = []
        for s in (2 * pair, 2 * pair + 1):
            tile = col_ref[s]
            start = pl.multiple_of((tile // 2) * (2 * width), 2 * width)
            both = coef_ref[:, pl.ds(start, 2 * width)].astype(jnp.float32)
            want = s % 2
            swapped = pltpu.roll(both, width, 1)
            keep = jnp.full(both.shape, tile % 2, jnp.int32) == want
            live = jnp.full(both.shape, s, jnp.int32) < count_ref[0]
            halves.append(jnp.where(live, jnp.where(keep, both, swapped), 0.0))
        lane = lax.broadcasted_iota(jnp.int32, halves[0].shape, 1)
        merged = jnp.where(lane < width, halves[0], halves[1]).astype(out_ref.dtype)
        for n in range(copies):
            out_ref[n, :, pair * 2 * width : (pair + 1) * 2 * width] = merged


def pick(coefficients, cols, count, copies, width):
    norb = coefficients.shape[0]
    slots = cols.shape[0]
    return pl.pallas_call(
        functools.partial(pick_kernel, copies, width),
        out_shape=jax.ShapeDtypeStruct((copies, norb, slots * width), coefficients.dtype),
        in_specs=[
            pl.BlockSpec(memory_space=pltpu.SMEM),
            pl.BlockSpec(memory_space=pltpu.SMEM),
            pl.BlockSpec(memory_space=pltpu.VMEM),
        ],
        out_specs=pl.BlockSpec(memory_space=pltpu.VMEM),
        name="pick",
    )(cols, count, coefficients)


def exchange_kernel(ncore, naux, core_ref, own_ref, other_ref, picked_ref, keep_ref, send_ref, half, total):
    t = pl.program_id(0)
    ntiles = pl.num_programs(0)
    _, nq, height, width = own_ref.shape
    norb = picked_ref.shape[0] * picked_ref.shape[2] * picked_ref.shape[3]
    picked = picked_ref[...].reshape(norb, width)
    start = pl.multiple_of(t * height, height)
    for block, ref in enumerate((own_ref, other_ref)):
        result = lax.dot_general(
            ref[...].reshape(nq * height, width),
            picked,
            (((1,), (1,)), ((), ())),
            preferred_element_type=jnp.float32,
        ).astype(jnp.bfloat16)
        for q in range(nq):
            col = (block * nq + q) * norb
            half[pl.ds(start, height), col : col + norb] = result[q * height : (q + 1) * height]

    @pl.when(t == ntiles - 1)
    def _():
        rows = total.shape[0]
        step = rows // 2
        for i in range(2):
            for j in range(2):
                total[i * step : (i + 1) * step, j * step : (j + 1) * step] = lax.dot_general(
                    half[i * step : (i + 1) * step, :],
                    half[j * step : (j + 1) * step, :],
                    (((1,), (1,)), ((), ())),
                    preferred_element_type=jnp.float32,
                )
        whole = total[...]
        on_diagonal = lax.broadcasted_iota(jnp.int32, whole.shape, 0) == lax.broadcasted_iota(
            jnp.int32, whole.shape, 1
        )
        diagonal = jnp.sum(jnp.where(on_diagonal, whole, 0.0), axis=0, keepdims=True)
        cols = rows // naux
        nrow = rows // height
        hc = cols // 2
        low = lax.broadcasted_iota(jnp.int32, (hc, 2 * height), 1) < height
        low1 = lax.broadcasted_iota(jnp.int32, (1, 2 * height), 1) < height
        per = hc + 1
        for which, out_ref in ((0, keep_ref), (1, send_ref)):
            core = core_ref[0] if which == 0 else 1 - core_ref[0]
            for a in range(naux // ncore):
                first = pl.multiple_of((a * ncore + core) * cols, cols)
                for pair in range(nrow // 2):
                    lanes = slice(pair * 2 * height, (pair + 1) * 2 * height)
                    top = total[pl.ds(first, hc), lanes]
                    bottom = total[pl.ds(pl.multiple_of(first + hc, hc), hc), lanes]
                    d = diagonal[:, lanes]
                    even = jnp.where(low, top, pltpu.roll(bottom, height, 1))
                    odd = jnp.where(low, pltpu.roll(top, height, 1), bottom)
                    base = (a * nrow + 2 * pair) * per
                    out_ref[base : base + hc, :] = even
                    out_ref[base + hc : base + per, :] = jnp.where(low1, d, 0.0)
                    out_ref[base + per : base + per + hc, :] = odd
                    out_ref[base + per + hc : base + 2 * per, :] = jnp.where(low1, pltpu.roll(d, height, 1), 0.0)


def exchange(core, own, other, picked, ncore, naux):
    ntiles, nq, height, width = own.shape
    nz, _, nxl, norb, _ = picked.shape
    rows = ntiles * height
    cols = rows // naux
    messages = (naux // ncore) * ntiles
    shape = jax.ShapeDtypeStruct((messages * (cols // 2 + 1), 2 * height), jnp.float32)
    all_orb = nz * nxl * norb
    return pl.pallas_call(
        functools.partial(exchange_kernel, ncore, naux),
        out_shape=(shape, shape),
        grid_spec=pltpu.PrefetchScalarGridSpec(
            num_scalar_prefetch=1,
            grid=(ntiles,),
            in_specs=[
                pl.BlockSpec((1, nq, height, width), lambda t, c: (t, 0, 0, 0)),
                pl.BlockSpec((1, nq, height, width), lambda t, c: (t, 0, 0, 0)),
                pl.BlockSpec((nz, 1, nxl, norb, width), lambda t, c: (0, t, 0, 0, 0)),
            ],
            out_specs=[pl.BlockSpec(shape.shape, lambda t, c: (0, 0))] * 2,
            scratch_shapes=[
                pltpu.VMEM((rows, 2 * nq * all_orb), jnp.bfloat16),
                pltpu.VMEM((rows, rows), jnp.float32),
            ],
        ),
        compiler_params=pltpu.CompilerParams(
            dimension_semantics=("arbitrary",), vmem_limit_bytes=56 * 1024 * 1024
        ),
        cost_estimate=pl.CostEstimate(
            flops=4 * nq * rows * all_orb * (width + rows), bytes_accessed=12 << 20, transcendentals=0
        ),
        name="exchange",
    )(core, own, other, picked)


def finish_kernel(scale_diagonal, scale_tiles, per, place_ref, got_ref, tiles_ref, diagonal_ref):
    messages = got_ref.shape[0] // per
    hc = per - 1
    cols, height = tiles_ref.shape
    total = got_ref[0:per, :]
    for n in range(1, messages):
        total = total + got_ref[n * per : (n + 1) * per, :]
    top = total[:hc]
    flat = jnp.concatenate([top, pltpu.roll(top, height, 1)], axis=0)[:, :height]
    n = place_ref[1] * cols + lax.broadcasted_iota(jnp.int32, flat.shape, 0)
    m = place_ref[0] * height + lax.broadcasted_iota(jnp.int32, flat.shape, 1)
    tiles_ref[...] = jnp.where(m == n, 0.0, flat) / scale_tiles
    diagonal_ref[...] = total[hc:per, :height] / scale_diagonal


def finish(got, place, height, cols, count):
    per = cols // 2 + 1
    return pl.pallas_call(
        functools.partial(finish_kernel, float(count), float(count) ** 0.5, per),
        out_shape=(
            jax.ShapeDtypeStruct((cols, height), jnp.float32),
            jax.ShapeDtypeStruct((1, height), jnp.float32),
        ),
        in_specs=[pl.BlockSpec(memory_space=pltpu.SMEM), pl.BlockSpec(memory_space=pltpu.VMEM)],
        out_specs=[pl.BlockSpec(memory_space=pltpu.VMEM)] * 2,
        name="finish",
    )(place, got)


def local(three_center, coefficients, col_tiles, tile_count):
    nq, _, height, width = three_center.shape
    nz, nxl, ncore = (lax.axis_size(a) for a in AUX)
    nrow = lax.axis_size("y") * lax.axis_size("xh")
    naux = nz * nxl * ncore
    norb = coefficients.shape[0]
    rows = nrow * height
    cols = rows // naux
    core = lax.axis_index("c")

    picks = pick(coefficients, col_tiles.reshape(-1), tile_count, nrow * nxl, height)
    picks = lax.all_to_all(picks, ROW + ("xl",), 0, 0, tiled=True)
    picked = lax.all_gather(picks, "z", axis=0, tiled=True)
    picked = picked.reshape(nz, nrow, nxl, norb, width)

    integrals = three_center.reshape(nq, height, width)
    integrals, picks = lax.optimization_barrier((integrals, picks))
    own = lax.all_to_all(integrals, ROW, 0, 0, tiled=True)
    own = own.reshape(nrow, nq // nrow, height, width)
    other = lax.ppermute(own, "c", [(0, 1), (1, 0)])

    keep, send = exchange(core.reshape(1), own, other, picked, ncore, naux)
    mine = keep + lax.ppermute(send, "c", [(0, 1), (1, 0)])
    got = lax.all_to_all(mine, ("z", "xl") + ROW, 0, 0, tiled=True)

    row = lax.axis_index(ROW)
    place = jnp.stack([row, lax.axis_index(AUX)]).astype(jnp.int32)
    tiles, diagonal = finish(got, place, height, cols, nq * naux * norb * naux)
    return tiles.T, diagonal.reshape(height)


def solution(mesh):
    fine = Mesh(mesh.devices.reshape(8, 2, 2, 4, 2), AUX + ROW)
    in_specs = (P(AUX, ROW, None, None), P(AUX, None), P(ROW, None), P(ROW))
    out_specs = (P(ROW, AUX), P(ROW))
    return jax.shard_map(local, mesh=fine, in_specs=in_specs, out_specs=out_specs, check_vma=False)
```

```python
import functools

import jax
import jax.numpy as jnp
from jax import lax
from jax.experimental import pallas as pl
from jax.experimental.pallas import tpu as pltpu
from jax.sharding import Mesh, PartitionSpec as P

ROW = ("y", "xh")
AUX = ("z", "xl", "c")


def pick_kernel(copies, width, col_ref, count_ref, coef_ref, out_ref):
    slots = col_ref.shape[0]
    for pair in range(slots // 2):
        halves = []
        for s in (2 * pair, 2 * pair + 1):
            tile = col_ref[s]
            start = pl.multiple_of((tile // 2) * (2 * width), 2 * width)
            both = coef_ref[:, pl.ds(start, 2 * width)].astype(jnp.float32)
            want = s % 2
            swapped = pltpu.roll(both, width, 1)
            keep = jnp.full(both.shape, tile % 2, jnp.int32) == want
            live = jnp.full(both.shape, s, jnp.int32) < count_ref[0]
            halves.append(jnp.where(live, jnp.where(keep, both, swapped), 0.0))
        lane = lax.broadcasted_iota(jnp.int32, halves[0].shape, 1)
        merged = jnp.where(lane < width, halves[0], halves[1]).astype(out_ref.dtype)
        for n in range(copies):
            out_ref[n, :, pair * 2 * width : (pair + 1) * 2 * width] = merged


def pick(coefficients, cols, count, copies, width):
    norb = coefficients.shape[0]
    slots = cols.shape[0]
    return pl.pallas_call(
        functools.partial(pick_kernel, copies, width),
        out_shape=jax.ShapeDtypeStruct((copies, norb, slots * width), coefficients.dtype),
        in_specs=[
            pl.BlockSpec(memory_space=pltpu.SMEM),
            pl.BlockSpec(memory_space=pltpu.SMEM),
            pl.BlockSpec(memory_space=pltpu.VMEM),
        ],
        out_specs=pl.BlockSpec(memory_space=pltpu.VMEM),
        name="pick",
    )(cols, count, coefficients)


def gather_half(own_ref, other_ref, blocks, held, sem, half):
    ntiles, nq, height, width = own_ref.shape
    norb = len(blocks) * blocks[0].shape[1]
    copies = [pltpu.make_async_copy(ref, held.at[n], sem.at[n]) for n, ref in enumerate(blocks)]
    for copy in copies:
        copy.start()
    for copy in copies:
        copy.wait()

    def tile(t, _):
        picked = held[:, t].reshape(norb, width)
        start = pl.multiple_of(t * height, height)
        for block, ref in enumerate((own_ref, other_ref)):
            result = lax.dot_general(
                ref[t].reshape(nq * height, width),
                picked,
                (((1,), (1,)), ((), ())),
                preferred_element_type=jnp.float32,
            ).astype(jnp.bfloat16)
            for q in range(nq):
                col = (block * nq + q) * norb
                half[pl.ds(start, height), col : col + norb] = result[q * height : (q + 1) * height]
        return 0

    lax.fori_loop(0, ntiles, tile, 0)


def product(half, i, j, step):
    return lax.dot_general(
        half[i * step : (i + 1) * step, :],
        half[j * step : (j + 1) * step, :],
        (((1,), (1,)), ((), ())),
        preferred_element_type=jnp.float32,
    )


def early_kernel(own_ref, other_ref, *refs):
    *blocks, total_ref, held, sem, half = refs
    gather_half(own_ref, other_ref, blocks, held, sem, half)
    step = total_ref.shape[0] // 2
    for i, j in ((0, 0), (1, 1), (1, 0)):
        total_ref[i * step : (i + 1) * step, j * step : (j + 1) * step] = product(half, i, j, step)


def late_kernel(ncore, naux, core_ref, own_ref, other_ref, early_ref, *refs):
    *blocks, keep_ref, send_ref, held, sem, half, total = refs
    gather_half(own_ref, other_ref, blocks, held, sem, half)
    rows = total.shape[0]
    height = own_ref.shape[2]
    step = rows // 2
    for i, j in ((0, 0), (1, 1), (1, 0)):
        rest = early_ref[i * step : (i + 1) * step, j * step : (j + 1) * step]
        block = product(half, i, j, step) + rest
        total[i * step : (i + 1) * step, j * step : (j + 1) * step] = block
        if i != j:
            total[j * step : (j + 1) * step, i * step : (i + 1) * step] = block.T
    whole = total[...]
    on_diagonal = lax.broadcasted_iota(jnp.int32, whole.shape, 0) == lax.broadcasted_iota(
        jnp.int32, whole.shape, 1
    )
    diagonal = jnp.sum(jnp.where(on_diagonal, whole, 0.0), axis=0, keepdims=True)
    cols = rows // naux
    nrow = rows // height
    hc = cols // 2
    low = lax.broadcasted_iota(jnp.int32, (hc, 2 * height), 1) < height
    low1 = lax.broadcasted_iota(jnp.int32, (1, 2 * height), 1) < height
    per = hc + 1
    for which, out_ref in ((0, keep_ref), (1, send_ref)):
        core = core_ref[0] if which == 0 else 1 - core_ref[0]
        for a in range(naux // ncore):
            first = pl.multiple_of((a * ncore + core) * cols, cols)
            for pair in range(nrow // 2):
                lanes = slice(pair * 2 * height, (pair + 1) * 2 * height)
                top = total[pl.ds(first, hc), lanes]
                bottom = total[pl.ds(pl.multiple_of(first + hc, hc), hc), lanes]
                d = diagonal[:, lanes]
                even = jnp.where(low, top, pltpu.roll(bottom, height, 1))
                odd = jnp.where(low, pltpu.roll(top, height, 1), bottom)
                base = (a * nrow + 2 * pair) * per
                out_ref[base : base + hc, :] = even
                out_ref[base + hc : base + per, :] = jnp.where(low1, d, 0.0)
                out_ref[base + per : base + per + hc, :] = odd
                out_ref[base + per + hc : base + 2 * per, :] = jnp.where(low1, pltpu.roll(d, height, 1), 0.0)


def exchange(core, own, other, early, late, ncore, naux):
    ntiles, nq, height, width = own.shape
    norb = early[0].shape[1]
    rows = ntiles * height
    cols = rows // naux
    messages = (naux // ncore) * ntiles
    whole = pl.BlockSpec(memory_space=pltpu.VMEM)
    params = pltpu.CompilerParams(vmem_limit_bytes=32 * 1024 * 1024)
    own, other = (pltpu.with_memory_space_constraint(x, pltpu.VMEM) for x in (own, other))

    def cost(n):
        orb = n * norb
        return pl.CostEstimate(flops=4 * nq * rows * orb * (width + rows), bytes_accessed=1 << 20, transcendentals=0)

    def scratch(n):
        return [
            pltpu.VMEM((n, ntiles, norb, width), jnp.bfloat16),
            pltpu.SemaphoreType.DMA((n,)),
            pltpu.VMEM((rows, 2 * nq * n * norb), jnp.bfloat16),
        ]

    total = pl.pallas_call(
        early_kernel,
        out_shape=jax.ShapeDtypeStruct((rows, rows), jnp.float32),
        in_specs=[whole] * 2 + [pl.BlockSpec(memory_space=pl.ANY)] * len(early),
        out_specs=whole,
        scratch_shapes=scratch(len(early)),
        compiler_params=params,
        cost_estimate=cost(len(early)),
        name="early",
    )(own, other, *early)
    shape = jax.ShapeDtypeStruct((messages * (cols // 2 + 1), 2 * height), jnp.float32)
    return pl.pallas_call(
        functools.partial(late_kernel, ncore, naux),
        out_shape=(shape, shape),
        in_specs=[pl.BlockSpec(memory_space=pltpu.SMEM)] + [whole] * 3 + [pl.BlockSpec(memory_space=pl.ANY)] * len(late),
        out_specs=[whole] * 2,
        scratch_shapes=scratch(len(late)) + [pltpu.VMEM((rows, rows), jnp.float32)],
        compiler_params=params,
        cost_estimate=cost(len(late)),
        name="late",
    )(core, own, other, total, *late)


def ring(chunks, axis, size, beside, when):
    up = [(i, (i + 1) % size) for i in range(size)]
    down = [(i, (i - 1) % size) for i in range(size)]
    rights, lefts, got = list(chunks), list(chunks), []
    for step in range(1, size // 2 + 1):
        last = step == size // 2
        if step == when:
            rights, lefts, beside = lax.optimization_barrier((rights, lefts, beside))
        for n in range(len(chunks)):
            if not last or n % 2 == 0:
                rights[n] = lax.ppermute(rights[n], axis, up)
                got.append(rights[n])
            if not last or n % 2 == 1:
                lefts[n] = lax.ppermute(lefts[n], axis, down)
                got.append(lefts[n])
    return got, beside


def finish_kernel(scale_diagonal, scale_tiles, per, place_ref, got_ref, tiles_ref, diagonal_ref):
    messages = got_ref.shape[0] // per
    hc = per - 1
    cols, height = tiles_ref.shape
    total = got_ref[0:per, :]
    for n in range(1, messages):
        total = total + got_ref[n * per : (n + 1) * per, :]
    top = total[:hc]
    flat = jnp.concatenate([top, pltpu.roll(top, height, 1)], axis=0)[:, :height]
    n = place_ref[1] * cols + lax.broadcasted_iota(jnp.int32, flat.shape, 0)
    m = place_ref[0] * height + lax.broadcasted_iota(jnp.int32, flat.shape, 1)
    tiles_ref[...] = jnp.where(m == n, 0.0, flat) / scale_tiles
    diagonal_ref[...] = total[hc:per, :height] / scale_diagonal


def finish(got, place, height, cols, count):
    per = cols // 2 + 1
    return pl.pallas_call(
        functools.partial(finish_kernel, float(count), float(count) ** 0.5, per),
        out_shape=(
            jax.ShapeDtypeStruct((cols, height), jnp.float32),
            jax.ShapeDtypeStruct((1, height), jnp.float32),
        ),
        in_specs=[pl.BlockSpec(memory_space=pltpu.SMEM), pl.BlockSpec(memory_space=pltpu.VMEM)],
        out_specs=[pl.BlockSpec(memory_space=pltpu.VMEM)] * 2,
        name="finish",
    )(place, got)


def local(three_center, coefficients, col_tiles, tile_count):
    nq, _, height, width = three_center.shape
    nz, nxl, ncore = (lax.axis_size(a) for a in AUX)
    nrow = lax.axis_size("y") * lax.axis_size("xh")
    naux = nz * nxl * ncore
    norb = coefficients.shape[0]
    rows = nrow * height
    cols = rows // naux
    core = lax.axis_index("c")

    picks = pick(coefficients, col_tiles.reshape(-1), tile_count, nrow * nxl, height)
    integrals = three_center.reshape(nq, height, width)
    picks = lax.all_to_all(picks, ("xl",) + ROW, 0, 0, tiled=True)
    chunks = [picks[n * nrow : (n + 1) * nrow] for n in range(nxl)]
    own = lax.all_to_all(integrals, ROW, 0, 0, tiled=True)
    arrived, own = ring(chunks, "z", nz, own, 4)
    blocks = chunks + arrived
    own = own.reshape(nrow, nq // nrow, height, width)
    other = lax.ppermute(own, "c", [(0, 1), (1, 0)])

    early = len(blocks) // 2
    blocks = [pltpu.with_memory_space_constraint(b, pltpu.HBM) for b in blocks]
    keep, send = exchange(core.reshape(1), own, other, blocks[:early], blocks[early:], ncore, naux)
    mine = keep + lax.ppermute(send, "c", [(0, 1), (1, 0)])
    mine = mine.reshape(mine.shape[0], 1, mine.shape[1])
    got = lax.all_to_all(mine, ("z", "xl") + ROW, 0, 0, tiled=True)
    got = pltpu.with_memory_space_constraint(got.reshape(got.shape[0], got.shape[2]), pltpu.VMEM)

    row = lax.axis_index(ROW)
    place = jnp.stack([row, lax.axis_index(AUX)]).astype(jnp.int32)
    tiles, diagonal = finish(got, place, height, cols, nq * naux * norb * naux)
    return tiles.T, diagonal.reshape(height)


def solution(mesh):
    fine = Mesh(mesh.devices.reshape(8, 2, 2, 4, 2), AUX + ROW)
    in_specs = (P(AUX, ROW, None, None), P(AUX, None), P(ROW, None), P(ROW))
    out_specs = (P(ROW, AUX), P(ROW))
    return jax.shard_map(local, mesh=fine, in_specs=in_specs, out_specs=out_specs, check_vma=False)
```

```python
import functools

import jax
import jax.numpy as jnp
from jax import lax
from jax.experimental import pallas as pl
from jax.experimental.pallas import tpu as pltpu
from jax.sharding import Mesh, PartitionSpec as P

ROW = ("y", "xh")
AUX = ("z", "xl", "c")
A_PASS = 8
UNROLL = 4


def pick_kernel(copies, width, col_ref, count_ref, coef_ref, out_ref):
    slots = col_ref.shape[0]
    for pair in range(slots // 2):
        halves = []
        for s in (2 * pair, 2 * pair + 1):
            tile = col_ref[s]
            start = pl.multiple_of((tile // 2) * (2 * width), 2 * width)
            both = coef_ref[:, pl.ds(start, 2 * width)].astype(jnp.float32)
            want = s % 2
            swapped = pltpu.roll(both, width, 1)
            keep = jnp.full(both.shape, tile % 2, jnp.int32) == want
            live = jnp.full(both.shape, s, jnp.int32) < count_ref[0]
            halves.append(jnp.where(live, jnp.where(keep, both, swapped), 0.0))
        lane = lax.broadcasted_iota(jnp.int32, halves[0].shape, 1)
        merged = jnp.where(lane < width, halves[0], halves[1]).astype(out_ref.dtype)
        for n in range(copies):
            out_ref[n, :, pair * 2 * width : (pair + 1) * 2 * width] = merged


def pick(coefficients, cols, count, copies, width):
    norb = coefficients.shape[0]
    slots = cols.shape[0]
    return pl.pallas_call(
        functools.partial(pick_kernel, copies, width),
        out_shape=jax.ShapeDtypeStruct((copies, norb, slots * width), coefficients.dtype),
        in_specs=[
            pl.BlockSpec(memory_space=pltpu.SMEM),
            pl.BlockSpec(memory_space=pltpu.SMEM),
            pl.BlockSpec(memory_space=pltpu.VMEM),
        ],
        out_specs=pl.BlockSpec(memory_space=pltpu.VMEM),
        name="pick",
    )(cols, count, coefficients)


def half_rows(part, pieces, base, half, tiles):
    _, nq, height, width = part.shape
    orbitals = sum(piece.shape[0] * piece.shape[2] for piece in pieces)

    def tile(t, _):
        start = pl.multiple_of(t * height, height)
        picked = [piece[:, t].reshape(-1, width) for piece in pieces]
        result = lax.dot_general(
            part[t].reshape(nq * height, width),
            picked[0] if len(picked) == 1 else jnp.concatenate(picked, axis=0),
            (((1,), (1,)), ((), ())),
            preferred_element_type=jnp.float32,
        ).astype(jnp.bfloat16)
        for q in range(nq):
            col = base + q * orbitals
            half[pl.ds(start, height), col : col + orbitals] = result[q * height : (q + 1) * height]
        return 0

    lax.fori_loop(tiles[0], tiles[1], tile, 0, unroll=UNROLL)
    return base + nq * orbitals


def copies_of(blocks, held, sem):
    copies = [pltpu.make_async_copy(ref, held.at[n], sem.at[n]) for n, ref in enumerate(blocks)]
    for copy in copies:
        copy.start()
    return copies


def lower_products(half, add):
    step = half.shape[0] // 2
    for i, j in ((0, 0), (1, 1), (1, 0)):
        rows, cols = slice(i * step, (i + 1) * step), slice(j * step, (j + 1) * step)
        add(
            rows,
            cols,
            lax.dot_general(
                half[rows, :], half[cols, :], (((1,), (1,)), ((), ())), preferred_element_type=jnp.float32
            ),
        )


def early_kernel(own_ref, *refs):
    *blocks, total_ref, held, sem, half = refs
    copies = copies_of(blocks, held, sem)
    base = 0
    for low in range(0, len(blocks), A_PASS):
        high = min(low + A_PASS, len(blocks))
        for copy in copies[low:high]:
            copy.wait()
        base = half_rows(own_ref, [held.at[low:high]], base, half, (0, own_ref.shape[0]))

    def add(rows, cols, block):
        total_ref[rows, cols] = block

    lower_products(half, add)


def late_kernel(nz, nxl, ncore, core_ref, own_ref, early_ref, held, other_ref, *refs):
    *blocks, keep_ref, send_ref, other, other_sem, last, sem, half, total = refs
    rows = total.shape[0]
    ntiles, nq, height, _ = own_ref.shape
    copies = copies_of(blocks, last, sem)
    parts = [pltpu.make_async_copy(other_ref.at[t], other.at[t], other_sem.at[t]) for t in range(ntiles)]
    for copy in parts:
        copy.start()
    for copy in copies:
        copy.wait()
    base = half_rows(own_ref, [last], 0, half, (0, ntiles))
    for low in range(0, ntiles, UNROLL):
        tiles = (low, low + UNROLL)
        for copy in parts[low : low + UNROLL]:
            copy.wait()
        middle = half_rows(other, [held.at[:A_PASS]], base, half, tiles)
        half_rows(other, [held.at[A_PASS : held.shape[0]], last], middle, half, tiles)

    def add(rows, cols, block):
        block = block + early_ref[rows, cols]
        total[rows, cols] = block
        if rows != cols:
            total[cols, rows] = block.T

    lower_products(half, add)
    whole = total[...]
    on_diagonal = lax.broadcasted_iota(jnp.int32, whole.shape, 0) == lax.broadcasted_iota(
        jnp.int32, whole.shape, 1
    )
    diagonal = jnp.sum(jnp.where(on_diagonal, whole, 0.0), axis=0, keepdims=True)
    cols = rows // (nz * nxl * ncore)
    nrow = rows // height
    hc = cols // 2
    low = lax.broadcasted_iota(jnp.int32, (hc, 2 * height), 1) < height
    low1 = lax.broadcasted_iota(jnp.int32, (1, 2 * height), 1) < height
    per = hc + 1
    for which, out_ref in ((0, keep_ref), (1, send_ref)):
        core = core_ref[0] if which == 0 else 1 - core_ref[0]
        for z in range(nz):
            for x in range(nxl):
                first = pl.multiple_of(((z * nxl + x) * ncore + core) * cols, cols)
                for pair in range(nrow // 2):
                    lanes = slice(pair * 2 * height, (pair + 1) * 2 * height)
                    top = total[pl.ds(first, hc), lanes]
                    bottom = total[pl.ds(pl.multiple_of(first + hc, hc), hc), lanes]
                    d = diagonal[:, lanes]
                    even = jnp.where(low, top, pltpu.roll(bottom, height, 1))
                    odd = jnp.where(low, pltpu.roll(top, height, 1), bottom)
                    base = ((x * nrow + 2 * pair) * nz + z) * per
                    out_ref[base : base + hc, :] = even
                    out_ref[base + hc : base + per, :] = jnp.where(low1, d, 0.0)
                    base += nz * per
                    out_ref[base : base + hc, :] = odd
                    out_ref[base + hc : base + per, :] = jnp.where(low1, pltpu.roll(d, height, 1), 0.0)


def exchange(core, own, other, blocks, rest, sizes):
    ntiles, nq, height, width = own.shape
    norb = blocks[0].shape[1]
    rows = ntiles * height
    nz, nxl, ncore = sizes
    cols = rows // (nz * nxl * ncore)
    messages = nz * nxl * ntiles
    count = len(blocks)
    whole = pl.BlockSpec(memory_space=pltpu.VMEM)
    blocks = [pltpu.with_memory_space_constraint(b, pltpu.HBM) for b in blocks[:rest]] + blocks[rest:]
    other = pltpu.with_memory_space_constraint(other, pltpu.HBM)
    own = pltpu.with_memory_space_constraint(own, pltpu.VMEM)

    def anywhere(n):
        return [pl.BlockSpec(memory_space=pl.ANY)] * n

    def settings(terms):
        return dict(
            compiler_params=pltpu.CompilerParams(vmem_limit_bytes=32 * 1024 * 1024),
            cost_estimate=pl.CostEstimate(
                flops=2 * nq * rows * terms * norb * (width + rows), bytes_accessed=1 << 20, transcendentals=0
            ),
        )

    total, held = pl.pallas_call(
        early_kernel,
        out_shape=(
            jax.ShapeDtypeStruct((rows, rows), jnp.float32),
            jax.ShapeDtypeStruct((rest, ntiles, norb, width), jnp.bfloat16),
        ),
        in_specs=[whole] + anywhere(rest),
        out_specs=[whole] * 2,
        scratch_shapes=[
            pltpu.SemaphoreType.DMA((rest,)),
            pltpu.VMEM((rows, nq * rest * norb), jnp.bfloat16),
        ],
        name="early",
        **settings(rest),
    )(own, *blocks[:rest])
    total = pltpu.with_memory_space_constraint(total, pltpu.VMEM)
    held = pltpu.with_memory_space_constraint(held, pltpu.VMEM)
    shape = jax.ShapeDtypeStruct((messages * (cols // 2 + 1), 2 * height), jnp.float32)
    terms = 2 * count - rest
    return pl.pallas_call(
        functools.partial(late_kernel, *sizes),
        out_shape=(shape, shape),
        in_specs=[pl.BlockSpec(memory_space=pltpu.SMEM)] + [whole] * 3 + anywhere(1 + count - rest),
        out_specs=[whole] * 2,
        scratch_shapes=[
            pltpu.VMEM(other.shape, other.dtype),
            pltpu.SemaphoreType.DMA((ntiles,)),
            pltpu.VMEM((count - rest, ntiles, norb, width), jnp.bfloat16),
            pltpu.SemaphoreType.DMA((count - rest,)),
            pltpu.VMEM((rows, nq * terms * norb), jnp.bfloat16),
            pltpu.VMEM((rows, rows), jnp.float32),
        ],
        name="late",
        **settings(terms),
    )(core, own, total, held, other, *blocks[rest:])


def ring(chunks, axis, size, beside, when):
    up = [(i, (i + 1) % size) for i in range(size)]
    down = [(i, (i - 1) % size) for i in range(size)]
    rights, lefts, got = list(chunks), list(chunks), []
    for step in range(1, size // 2 + 1):
        last = step == size // 2
        if step == when:
            rights, lefts, beside = lax.optimization_barrier((rights, lefts, beside))
        for n in range(len(chunks)):
            if not last or n % 2 == 0:
                rights[n] = lax.ppermute(rights[n], axis, up)
                got.append(rights[n])
            if not last or n % 2 == 1:
                lefts[n] = lax.ppermute(lefts[n], axis, down)
                got.append(lefts[n])
    return got, beside


def add_up(got_ref, per):
    total = got_ref[0:per, :]
    for n in range(1, got_ref.shape[0] // per):
        total = total + got_ref[n * per : (n + 1) * per, :]
    return total


def sum_kernel(got_ref, out_ref):
    out_ref[...] = add_up(got_ref, out_ref.shape[0])


def summed(got, parts):
    return pl.pallas_call(
        sum_kernel,
        out_shape=jax.ShapeDtypeStruct((got.shape[0] // parts, got.shape[1]), got.dtype),
        in_specs=[pl.BlockSpec(memory_space=pltpu.VMEM)],
        out_specs=pl.BlockSpec(memory_space=pltpu.VMEM),
        name="summed",
    )(pltpu.with_memory_space_constraint(got, pltpu.VMEM))


def finish_kernel(scale_diagonal, scale_tiles, per, place_ref, got_ref, tiles_ref, diagonal_ref):
    hc = per - 1
    cols, height = tiles_ref.shape
    total = add_up(got_ref, per)
    top = total[:hc]
    flat = jnp.concatenate([top, pltpu.roll(top, height, 1)], axis=0)[:, :height]
    n = place_ref[1] * cols + lax.broadcasted_iota(jnp.int32, flat.shape, 0)
    m = place_ref[0] * height + lax.broadcasted_iota(jnp.int32, flat.shape, 1)
    tiles_ref[...] = jnp.where(m == n, 0.0, flat) / scale_tiles
    diagonal_ref[...] = total[hc:per, :height] / scale_diagonal


def finish(got, place, height, cols, count):
    per = cols // 2 + 1
    return pl.pallas_call(
        functools.partial(finish_kernel, float(count), float(count) ** 0.5, per),
        out_shape=(
            jax.ShapeDtypeStruct((cols, height), jnp.float32),
            jax.ShapeDtypeStruct((1, height), jnp.float32),
        ),
        in_specs=[pl.BlockSpec(memory_space=pltpu.SMEM), pl.BlockSpec(memory_space=pltpu.VMEM)],
        out_specs=[pl.BlockSpec(memory_space=pltpu.VMEM)] * 2,
        name="finish",
    )(place, pltpu.with_memory_space_constraint(got, pltpu.VMEM))


def turn(rows, axes):
    rows = rows.reshape(rows.shape[0], 1, rows.shape[1])
    rows = lax.all_to_all(rows, axes, 0, 0, tiled=True)
    return rows.reshape(rows.shape[0], rows.shape[2])


def local(three_center, coefficients, col_tiles, tile_count):
    nq, _, height, width = three_center.shape
    nz, nxl, ncore = (lax.axis_size(a) for a in AUX)
    nrow = lax.axis_size("y") * lax.axis_size("xh")
    naux = nz * nxl * ncore
    norb = coefficients.shape[0]
    rows = nrow * height
    cols = rows // naux
    core = lax.axis_index("c")

    picks = pick(coefficients, col_tiles.reshape(-1), tile_count, nrow * nxl, height)
    integrals = three_center.reshape(nq, height, width)
    picks = lax.all_to_all(picks, ("xl",) + ROW, 0, 0, tiled=True)
    chunks = [picks[n * nrow : (n + 1) * nrow] for n in range(nxl)]
    own = lax.all_to_all(integrals, ROW, 0, 0, tiled=True)
    arrived, own = ring(chunks, "z", nz, own, 4)
    blocks = chunks + arrived
    own = own.reshape(nrow, nq // nrow, height, width)
    other = lax.ppermute(own, "c", [(0, 1), (1, 0)])

    keep, send = exchange(core.reshape(1), own, other, blocks, len(blocks) - nxl, (nz, nxl, ncore))
    mine = keep + lax.ppermute(send, "c", [(0, 1), (1, 0)])
    got = summed(turn(mine, ("xl",) + ROW), nrow * nxl)
    got = turn(got, "z")

    row = lax.axis_index(ROW)
    place = jnp.stack([row, lax.axis_index(AUX)]).astype(jnp.int32)
    tiles, diagonal = finish(got, place, height, cols, nq * naux * norb * naux)
    return tiles.T, diagonal.reshape(height)


def solution(mesh):
    fine = Mesh(mesh.devices.reshape(8, 2, 2, 4, 2), AUX + ROW)
    in_specs = (P(AUX, ROW, None, None), P(AUX, None), P(ROW, None), P(ROW))
    out_specs = (P(ROW, AUX), P(ROW))
    return jax.shard_map(local, mesh=fine, in_specs=in_specs, out_specs=out_specs, check_vma=False)
```

```python
import functools

import jax
import jax.numpy as jnp
from jax import lax
from jax.experimental import pallas as pl
from jax.experimental.pallas import tpu as pltpu
from jax.sharding import Mesh, PartitionSpec as P

ROW = ("y", "xh")
AUX = ("z", "xl", "c")
A_PASS = 8
UNROLL = 8


def pick_kernel(copies, width, col_ref, count_ref, coef_ref, out_ref):
    slots = col_ref.shape[0]
    for pair in range(slots // 2):
        halves = []
        for s in (2 * pair, 2 * pair + 1):
            tile = col_ref[s]
            start = pl.multiple_of((tile // 2) * (2 * width), 2 * width)
            both = coef_ref[:, pl.ds(start, 2 * width)].astype(jnp.float32)
            want = s % 2
            swapped = pltpu.roll(both, width, 1)
            keep = jnp.full(both.shape, tile % 2, jnp.int32) == want
            live = jnp.full(both.shape, s, jnp.int32) < count_ref[0]
            halves.append(jnp.where(live, jnp.where(keep, both, swapped), 0.0))
        lane = lax.broadcasted_iota(jnp.int32, halves[0].shape, 1)
        merged = jnp.where(lane < width, halves[0], halves[1]).astype(out_ref.dtype)
        for n in range(copies):
            out_ref[n, :, pair * 2 * width : (pair + 1) * 2 * width] = merged


def pick(coefficients, cols, count, copies, width):
    norb = coefficients.shape[0]
    slots = cols.shape[0]
    return pl.pallas_call(
        functools.partial(pick_kernel, copies, width),
        out_shape=jax.ShapeDtypeStruct((copies, norb, slots * width), coefficients.dtype),
        in_specs=[
            pl.BlockSpec(memory_space=pltpu.SMEM),
            pl.BlockSpec(memory_space=pltpu.SMEM),
            pl.BlockSpec(memory_space=pltpu.VMEM),
        ],
        out_specs=pl.BlockSpec(memory_space=pltpu.VMEM),
        name="pick",
    )(cols, count, coefficients)


def half_rows(part, pieces, base, half, tiles):
    _, nq, height, width = part.shape
    orbitals = sum(piece.shape[0] * piece.shape[2] for piece in pieces)

    def tile(t, _):
        start = pl.multiple_of(t * height, height)
        picked = [piece[:, t].reshape(-1, width) for piece in pieces]
        result = lax.dot_general(
            part[t].reshape(nq * height, width),
            picked[0] if len(picked) == 1 else jnp.concatenate(picked, axis=0),
            (((1,), (1,)), ((), ())),
            preferred_element_type=jnp.float32,
        ).astype(jnp.bfloat16)
        for q in range(nq):
            col = base + q * orbitals
            half[pl.ds(start, height), col : col + orbitals] = result[q * height : (q + 1) * height]
        return 0

    lax.fori_loop(tiles[0], tiles[1], tile, 0, unroll=UNROLL)
    return base + nq * orbitals


def copies_of(blocks, held, sem):
    copies = [pltpu.make_async_copy(ref, held.at[n], sem.at[n]) for n, ref in enumerate(blocks)]
    for copy in copies:
        copy.start()
    return copies


def lower_products(half, add):
    step = half.shape[0] // 2
    for i, j in ((0, 0), (1, 1), (1, 0)):
        rows, cols = slice(i * step, (i + 1) * step), slice(j * step, (j + 1) * step)
        add(
            rows,
            cols,
            lax.dot_general(
                half[rows, :], half[cols, :], (((1,), (1,)), ((), ())), preferred_element_type=jnp.float32
            ),
        )


def early_kernel(own_ref, *refs):
    *blocks, total_ref, held, sem, half = refs
    copies = copies_of(blocks, held, sem)
    base = 0
    for low in range(0, len(blocks), A_PASS):
        high = min(low + A_PASS, len(blocks))
        for copy in copies[low:high]:
            copy.wait()
        base = half_rows(own_ref, [held.at[low:high]], base, half, (0, own_ref.shape[0]))

    def add(rows, cols, block):
        total_ref[rows, cols] = block

    lower_products(half, add)


def late_kernel(nz, nxl, ncore, core_ref, own_ref, early_ref, held, other_ref, *refs):
    *blocks, keep_ref, send_ref, other, other_sem, last, sem, half, total = refs
    rows = total.shape[0]
    ntiles, nq, height, _ = own_ref.shape
    copies = copies_of(blocks, last, sem)
    parts = [pltpu.make_async_copy(other_ref.at[t], other.at[t], other_sem.at[t]) for t in range(ntiles)]
    for copy in parts:
        copy.start()
    for copy in copies:
        copy.wait()
    base = half_rows(own_ref, [last], 0, half, (0, ntiles))
    for low in range(0, ntiles, UNROLL):
        tiles = (low, low + UNROLL)
        for copy in parts[low : low + UNROLL]:
            copy.wait()
        middle = half_rows(other, [held.at[:A_PASS]], base, half, tiles)
        half_rows(other, [held.at[A_PASS : held.shape[0]], last], middle, half, tiles)

    def add(rows, cols, block):
        block = block + early_ref[rows, cols]
        total[rows, cols] = block
        if rows != cols:
            total[cols, rows] = block.T

    lower_products(half, add)
    whole = total[...]
    on_diagonal = lax.broadcasted_iota(jnp.int32, whole.shape, 0) == lax.broadcasted_iota(
        jnp.int32, whole.shape, 1
    )
    diagonal = jnp.sum(jnp.where(on_diagonal, whole, 0.0), axis=0, keepdims=True)
    cols = rows // (nz * nxl * ncore)
    nrow = rows // height
    hc = cols // 2
    low = lax.broadcasted_iota(jnp.int32, (hc, 2 * height), 1) < height
    low1 = lax.broadcasted_iota(jnp.int32, (1, 2 * height), 1) < height
    per = hc + 1
    for which, out_ref in ((0, keep_ref), (1, send_ref)):
        core = core_ref[0] if which == 0 else 1 - core_ref[0]
        for z in range(nz):
            for x in range(nxl):
                first = pl.multiple_of(((z * nxl + x) * ncore + core) * cols, cols)
                for pair in range(nrow // 2):
                    lanes = slice(pair * 2 * height, (pair + 1) * 2 * height)
                    top = total[pl.ds(first, hc), lanes]
                    bottom = total[pl.ds(pl.multiple_of(first + hc, hc), hc), lanes]
                    d = diagonal[:, lanes]
                    even = jnp.where(low, top, pltpu.roll(bottom, height, 1))
                    odd = jnp.where(low, pltpu.roll(top, height, 1), bottom)
                    base = ((x * nrow + 2 * pair) * nz + z) * per
                    out_ref[base : base + hc, :] = even
                    out_ref[base + hc : base + per, :] = jnp.where(low1, d, 0.0)
                    base += nz * per
                    out_ref[base : base + hc, :] = odd
                    out_ref[base + hc : base + per, :] = jnp.where(low1, pltpu.roll(d, height, 1), 0.0)


def exchange(core, own, other, blocks, rest, sizes):
    ntiles, nq, height, width = own.shape
    norb = blocks[0].shape[1]
    rows = ntiles * height
    nz, nxl, ncore = sizes
    cols = rows // (nz * nxl * ncore)
    messages = nz * nxl * ntiles
    count = len(blocks)
    whole = pl.BlockSpec(memory_space=pltpu.VMEM)
    blocks = [pltpu.with_memory_space_constraint(b, pltpu.HBM) for b in blocks[:rest]] + blocks[rest:]
    other = pltpu.with_memory_space_constraint(other, pltpu.HBM)
    own = pltpu.with_memory_space_constraint(own, pltpu.VMEM)

    def anywhere(n):
        return [pl.BlockSpec(memory_space=pl.ANY)] * n

    def settings(terms):
        return dict(
            compiler_params=pltpu.CompilerParams(vmem_limit_bytes=32 * 1024 * 1024),
            cost_estimate=pl.CostEstimate(
                flops=2 * nq * rows * terms * norb * (width + rows), bytes_accessed=1 << 20, transcendentals=0
            ),
        )

    total, held = pl.pallas_call(
        early_kernel,
        out_shape=(
            jax.ShapeDtypeStruct((rows, rows), jnp.float32),
            jax.ShapeDtypeStruct((rest, ntiles, norb, width), jnp.bfloat16),
        ),
        in_specs=[whole] + anywhere(rest),
        out_specs=[whole] * 2,
        scratch_shapes=[
            pltpu.SemaphoreType.DMA((rest,)),
            pltpu.VMEM((rows, nq * rest * norb), jnp.bfloat16),
        ],
        name="early",
        **settings(rest),
    )(own, *blocks[:rest])
    total = pltpu.with_memory_space_constraint(total, pltpu.VMEM)
    held = pltpu.with_memory_space_constraint(held, pltpu.VMEM)
    shape = jax.ShapeDtypeStruct((messages * (cols // 2 + 1), 2 * height), jnp.float32)
    terms = 2 * count - rest
    return pl.pallas_call(
        functools.partial(late_kernel, *sizes),
        out_shape=(shape, shape),
        in_specs=[pl.BlockSpec(memory_space=pltpu.SMEM)] + [whole] * 3 + anywhere(1 + count - rest),
        out_specs=[whole] * 2,
        scratch_shapes=[
            pltpu.VMEM(other.shape, other.dtype),
            pltpu.SemaphoreType.DMA((ntiles,)),
            pltpu.VMEM((count - rest, ntiles, norb, width), jnp.bfloat16),
            pltpu.SemaphoreType.DMA((count - rest,)),
            pltpu.VMEM((rows, nq * terms * norb), jnp.bfloat16),
            pltpu.VMEM((rows, rows), jnp.float32),
        ],
        name="late",
        **settings(terms),
    )(core, own, total, held, other, *blocks[rest:])


def ring(chunks, axis, size, beside, when):
    up = [(i, (i + 1) % size) for i in range(size)]
    down = [(i, (i - 1) % size) for i in range(size)]
    rights, lefts, got = list(chunks), list(chunks), []
    for step in range(1, size // 2 + 1):
        last = step == size // 2
        if step == when:
            rights, lefts, beside = lax.optimization_barrier((rights, lefts, beside))
        for n in range(len(chunks)):
            if not last or n % 2 == 0:
                rights[n] = lax.ppermute(rights[n], axis, up)
                got.append(rights[n])
            if not last or n % 2 == 1:
                lefts[n] = lax.ppermute(lefts[n], axis, down)
                got.append(lefts[n])
    return got, beside


def add_up(got_ref, per):
    total = got_ref[0:per, :]
    for n in range(1, got_ref.shape[0] // per):
        total = total + got_ref[n * per : (n + 1) * per, :]
    return total


def sum_kernel(got_ref, out_ref):
    out_ref[...] = add_up(got_ref, out_ref.shape[0])


def summed(got, parts):
    return pl.pallas_call(
        sum_kernel,
        out_shape=jax.ShapeDtypeStruct((got.shape[0] // parts, got.shape[1]), got.dtype),
        in_specs=[pl.BlockSpec(memory_space=pltpu.VMEM)],
        out_specs=pl.BlockSpec(memory_space=pltpu.VMEM),
        name="summed",
    )(pltpu.with_memory_space_constraint(got, pltpu.VMEM))


def finish_kernel(scale_diagonal, scale_tiles, per, place_ref, got_ref, tiles_ref, diagonal_ref):
    hc = per - 1
    cols, height = tiles_ref.shape
    total = add_up(got_ref, per)
    top = total[:hc]
    flat = jnp.concatenate([top, pltpu.roll(top, height, 1)], axis=0)[:, :height]
    n = place_ref[1] * cols + lax.broadcasted_iota(jnp.int32, flat.shape, 0)
    m = place_ref[0] * height + lax.broadcasted_iota(jnp.int32, flat.shape, 1)
    tiles_ref[...] = jnp.where(m == n, 0.0, flat) / scale_tiles
    diagonal_ref[...] = total[hc:per, :height] / scale_diagonal


def finish(got, place, height, cols, count):
    per = cols // 2 + 1
    return pl.pallas_call(
        functools.partial(finish_kernel, float(count), float(count) ** 0.5, per),
        out_shape=(
            jax.ShapeDtypeStruct((cols, height), jnp.float32),
            jax.ShapeDtypeStruct((1, height), jnp.float32),
        ),
        in_specs=[pl.BlockSpec(memory_space=pltpu.SMEM), pl.BlockSpec(memory_space=pltpu.VMEM)],
        out_specs=[pl.BlockSpec(memory_space=pltpu.VMEM)] * 2,
        name="finish",
    )(place, pltpu.with_memory_space_constraint(got, pltpu.VMEM))


def turn(rows, axes):
    rows = rows.reshape(rows.shape[0], 1, rows.shape[1])
    rows = lax.all_to_all(rows, axes, 0, 0, tiled=True)
    return rows.reshape(rows.shape[0], rows.shape[2])


def local(three_center, coefficients, col_tiles, tile_count):
    nq, _, height, width = three_center.shape
    nz, nxl, ncore = (lax.axis_size(a) for a in AUX)
    nrow = lax.axis_size("y") * lax.axis_size("xh")
    naux = nz * nxl * ncore
    norb = coefficients.shape[0]
    rows = nrow * height
    cols = rows // naux
    core = lax.axis_index("c")

    picks = pick(coefficients, col_tiles.reshape(-1), tile_count, nrow * nxl, height)
    integrals = three_center.reshape(nq, height, width)
    picks = lax.all_to_all(picks, ("xl",) + ROW, 0, 0, tiled=True)
    chunks = [picks[n * nrow : (n + 1) * nrow] for n in range(nxl)]
    integrals, chunks = lax.optimization_barrier((integrals, chunks))
    own = lax.all_to_all(integrals, ROW, 0, 0, tiled=True)
    arrived, own = ring(chunks, "z", nz, own, 4)
    blocks = chunks + arrived
    own = own.reshape(nrow, nq // nrow, height, width)
    other = lax.ppermute(own, "c", [(0, 1), (1, 0)])

    keep, send = exchange(core.reshape(1), own, other, blocks, len(blocks) - nxl, (nz, nxl, ncore))
    mine = keep + lax.ppermute(send, "c", [(0, 1), (1, 0)])
    got = summed(turn(mine, ("xl",) + ROW), nrow * nxl)
    got = turn(got, "z")

    row = lax.axis_index(ROW)
    place = jnp.stack([row, lax.axis_index(AUX)]).astype(jnp.int32)
    tiles, diagonal = finish(got, place, height, cols, nq * naux * norb * naux)
    return tiles.T, diagonal.reshape(height)


def solution(mesh):
    fine = Mesh(mesh.devices.reshape(8, 2, 2, 4, 2), AUX + ROW)
    in_specs = (P(AUX, ROW, None, None), P(AUX, None), P(ROW, None), P(ROW))
    out_specs = (P(ROW, AUX), P(ROW))
    return jax.shard_map(local, mesh=fine, in_specs=in_specs, out_specs=out_specs, check_vma=False)
```

```python
import functools

import jax
import jax.numpy as jnp
from jax import lax
from jax.experimental import pallas as pl
from jax.experimental.pallas import tpu as pltpu
from jax.sharding import Mesh, PartitionSpec as P

ROW = ("y", "xh")
AUX = ("z", "xl", "c")
A_PASS = 8
UNROLL = 8


def pick_kernel(copies, width, col_ref, count_ref, coef_ref, out_ref):
    slots = col_ref.shape[0]
    for pair in range(slots // 2):
        halves = []
        for s in (2 * pair, 2 * pair + 1):
            tile = col_ref[s]
            start = pl.multiple_of((tile // 2) * (2 * width), 2 * width)
            both = coef_ref[:, pl.ds(start, 2 * width)].astype(jnp.float32)
            want = s % 2
            swapped = pltpu.roll(both, width, 1)
            keep = jnp.full(both.shape, tile % 2, jnp.int32) == want
            live = jnp.full(both.shape, s, jnp.int32) < count_ref[0]
            halves.append(jnp.where(live, jnp.where(keep, both, swapped), 0.0))
        lane = lax.broadcasted_iota(jnp.int32, halves[0].shape, 1)
        merged = jnp.where(lane < width, halves[0], halves[1]).astype(out_ref.dtype)
        for n in range(copies):
            out_ref[n, :, pair * 2 * width : (pair + 1) * 2 * width] = merged


def pick(coefficients, cols, count, copies, width):
    norb = coefficients.shape[0]
    slots = cols.shape[0]
    return pl.pallas_call(
        functools.partial(pick_kernel, copies, width),
        out_shape=jax.ShapeDtypeStruct((copies, norb, slots * width), coefficients.dtype),
        in_specs=[
            pl.BlockSpec(memory_space=pltpu.SMEM),
            pl.BlockSpec(memory_space=pltpu.SMEM),
            pl.BlockSpec(memory_space=pltpu.VMEM),
        ],
        out_specs=pl.BlockSpec(memory_space=pltpu.VMEM),
        name="pick",
    )(cols, count, coefficients)


def half_rows(part, pieces, base, half, tiles):
    _, nq, height, width = part.shape
    orbitals = sum(piece.shape[0] * piece.shape[2] for piece in pieces)

    def tile(t, _):
        start = pl.multiple_of(t * height, height)
        picked = [piece[:, t].reshape(-1, width) for piece in pieces]
        result = lax.dot_general(
            part[t].reshape(nq * height, width),
            picked[0] if len(picked) == 1 else jnp.concatenate(picked, axis=0),
            (((1,), (1,)), ((), ())),
            preferred_element_type=jnp.float32,
        ).astype(jnp.bfloat16)
        for q in range(nq):
            col = base + q * orbitals
            half[pl.ds(start, height), col : col + orbitals] = result[q * height : (q + 1) * height]
        return 0

    lax.fori_loop(tiles[0], tiles[1], tile, 0, unroll=UNROLL)
    return base + nq * orbitals


def copies_of(blocks, held, sem):
    copies = [pltpu.make_async_copy(ref, held.at[n], sem.at[n]) for n, ref in enumerate(blocks)]
    for copy in copies:
        copy.start()
    return copies


def lower_products(half, add):
    step = half.shape[0] // 2
    for i, j in ((0, 0), (1, 1), (1, 0)):
        rows, cols = slice(i * step, (i + 1) * step), slice(j * step, (j + 1) * step)
        add(
            rows,
            cols,
            lax.dot_general(
                half[rows, :], half[cols, :], (((1,), (1,)), ((), ())), preferred_element_type=jnp.float32
            ),
        )


def early_kernel(own_ref, *refs):
    *blocks, total_ref, held, sem, half = refs
    copies = copies_of(blocks, held, sem)
    base = 0
    for low in range(0, len(blocks), A_PASS):
        high = min(low + A_PASS, len(blocks))
        for copy in copies[low:high]:
            copy.wait()
        base = half_rows(own_ref, [held.at[low:high]], base, half, (0, own_ref.shape[0]))

    def add(rows, cols, block):
        total_ref[rows, cols] = block

    lower_products(half, add)


def middle_kernel(early_ref, held, other_ref, total_ref, other, sem, half):
    ntiles = other.shape[0]
    parts = [pltpu.make_async_copy(other_ref.at[t], other.at[t], sem.at[t]) for t in range(ntiles)]
    for copy in parts:
        copy.start()
    for low in range(0, ntiles, ntiles // 2):
        for copy in parts[low : low + ntiles // 2]:
            copy.wait()
        half_rows(other, [held.at[:A_PASS]], 0, half, (low, low + ntiles // 2))

    def add(rows, cols, block):
        total_ref[rows, cols] = block + early_ref[rows, cols]

    lower_products(half, add)


def late_kernel(nz, nxl, ncore, core_ref, own_ref, early_ref, held, other_ref, *refs):
    *blocks, keep_ref, send_ref, last, sem, half, total = refs
    rows = total.shape[0]
    ntiles, _, height, _ = own_ref.shape
    copies = copies_of(blocks, last, sem)
    everything = (0, ntiles)
    for copy in copies:
        copy.wait()
    base = half_rows(own_ref, [last], 0, half, everything)
    half_rows(other_ref, [held.at[A_PASS : held.shape[0]], last], base, half, everything)

    def add(rows, cols, block):
        block = block + early_ref[rows, cols]
        total[rows, cols] = block
        if rows != cols:
            total[cols, rows] = block.T

    lower_products(half, add)
    whole = total[...]
    on_diagonal = lax.broadcasted_iota(jnp.int32, whole.shape, 0) == lax.broadcasted_iota(
        jnp.int32, whole.shape, 1
    )
    diagonal = jnp.sum(jnp.where(on_diagonal, whole, 0.0), axis=0, keepdims=True)
    cols = rows // (nz * nxl * ncore)
    nrow = rows // height
    hc = cols // 2
    low = lax.broadcasted_iota(jnp.int32, (hc, 2 * height), 1) < height
    low1 = lax.broadcasted_iota(jnp.int32, (1, 2 * height), 1) < height
    per = hc + 1
    for which, out_ref in ((0, keep_ref), (1, send_ref)):
        core = core_ref[0] if which == 0 else 1 - core_ref[0]
        for z in range(nz):
            for x in range(nxl):
                first = pl.multiple_of(((z * nxl + x) * ncore + core) * cols, cols)
                for pair in range(nrow // 2):
                    lanes = slice(pair * 2 * height, (pair + 1) * 2 * height)
                    top = total[pl.ds(first, hc), lanes]
                    bottom = total[pl.ds(pl.multiple_of(first + hc, hc), hc), lanes]
                    d = diagonal[:, lanes]
                    even = jnp.where(low, top, pltpu.roll(bottom, height, 1))
                    odd = jnp.where(low, pltpu.roll(top, height, 1), bottom)
                    base = ((x * nrow + 2 * pair) * nz + z) * per
                    out_ref[base : base + hc, :] = even
                    out_ref[base + hc : base + per, :] = jnp.where(low1, d, 0.0)
                    base += nz * per
                    out_ref[base : base + hc, :] = odd
                    out_ref[base + hc : base + per, :] = jnp.where(low1, pltpu.roll(d, height, 1), 0.0)


def exchange(core, own, other, blocks, rest, sizes):
    ntiles, nq, height, width = own.shape
    norb = blocks[0].shape[1]
    rows = ntiles * height
    nz, nxl, ncore = sizes
    cols = rows // (nz * nxl * ncore)
    messages = nz * nxl * ntiles
    count = len(blocks)
    whole = pl.BlockSpec(memory_space=pltpu.VMEM)
    blocks = [pltpu.with_memory_space_constraint(b, pltpu.HBM) for b in blocks[:rest]] + blocks[rest:]
    other = pltpu.with_memory_space_constraint(other, pltpu.HBM)
    own = pltpu.with_memory_space_constraint(own, pltpu.VMEM)

    def anywhere(n):
        return [pl.BlockSpec(memory_space=pl.ANY)] * n

    def settings(terms):
        return dict(
            compiler_params=pltpu.CompilerParams(vmem_limit_bytes=32 * 1024 * 1024),
            cost_estimate=pl.CostEstimate(
                flops=2 * nq * rows * terms * norb * (width + rows), bytes_accessed=1 << 20, transcendentals=0
            ),
        )

    total, held = pl.pallas_call(
        early_kernel,
        out_shape=(
            jax.ShapeDtypeStruct((rows, rows), jnp.float32),
            jax.ShapeDtypeStruct((rest, ntiles, norb, width), jnp.bfloat16),
        ),
        in_specs=[whole] + anywhere(rest),
        out_specs=[whole] * 2,
        scratch_shapes=[
            pltpu.SemaphoreType.DMA((rest,)),
            pltpu.VMEM((rows, nq * rest * norb), jnp.bfloat16),
        ],
        name="early",
        **settings(rest),
    )(own, *blocks[:rest])
    total = pltpu.with_memory_space_constraint(total, pltpu.VMEM)
    held = pltpu.with_memory_space_constraint(held, pltpu.VMEM)
    total, other = pl.pallas_call(
        middle_kernel,
        out_shape=(jax.ShapeDtypeStruct(total.shape, total.dtype), jax.ShapeDtypeStruct(other.shape, other.dtype)),
        in_specs=[whole] * 2 + anywhere(1),
        out_specs=[whole] * 2,
        scratch_shapes=[
            pltpu.SemaphoreType.DMA((ntiles,)),
            pltpu.VMEM((rows, nq * A_PASS * norb), jnp.bfloat16),
        ],
        name="middle",
        **settings(A_PASS),
    )(total, held, other)
    total = pltpu.with_memory_space_constraint(total, pltpu.VMEM)
    other = pltpu.with_memory_space_constraint(other, pltpu.VMEM)
    shape = jax.ShapeDtypeStruct((messages * (cols // 2 + 1), 2 * height), jnp.float32)
    terms = 2 * count - rest - A_PASS
    return pl.pallas_call(
        functools.partial(late_kernel, *sizes),
        out_shape=(shape, shape),
        in_specs=[pl.BlockSpec(memory_space=pltpu.SMEM)] + [whole] * 4 + anywhere(count - rest),
        out_specs=[whole] * 2,
        scratch_shapes=[
            pltpu.VMEM((count - rest, ntiles, norb, width), jnp.bfloat16),
            pltpu.SemaphoreType.DMA((count - rest,)),
            pltpu.VMEM((rows, nq * terms * norb), jnp.bfloat16),
            pltpu.VMEM((rows, rows), jnp.float32),
        ],
        name="late",
        **settings(terms),
    )(core, own, total, held, other, *blocks[rest:])


def ring(chunks, axis, size, beside, when):
    up = [(i, (i + 1) % size) for i in range(size)]
    down = [(i, (i - 1) % size) for i in range(size)]
    rights, lefts, got = list(chunks), list(chunks), []
    for step in range(1, size // 2 + 1):
        last = step == size // 2
        for n in range(len(chunks)):
            if not last or n % 2 == 0:
                rights[n] = lax.ppermute(rights[n], axis, up)
                got.append(rights[n])
            if not last or n % 2 == 1:
                lefts[n] = lax.ppermute(lefts[n], axis, down)
                got.append(lefts[n])
        if step == when:
            *got, beside = lax.optimization_barrier((*got, beside))
    return got, beside


def add_up(got_ref, per):
    total = got_ref[0:per, :]
    for n in range(1, got_ref.shape[0] // per):
        total = total + got_ref[n * per : (n + 1) * per, :]
    return total


def sum_kernel(got_ref, out_ref):
    out_ref[...] = add_up(got_ref, out_ref.shape[0])


def summed(got, parts):
    return pl.pallas_call(
        sum_kernel,
        out_shape=jax.ShapeDtypeStruct((got.shape[0] // parts, got.shape[1]), got.dtype),
        in_specs=[pl.BlockSpec(memory_space=pltpu.VMEM)],
        out_specs=pl.BlockSpec(memory_space=pltpu.VMEM),
        name="summed",
    )(pltpu.with_memory_space_constraint(got, pltpu.VMEM))


def finish_kernel(scale_diagonal, scale_tiles, per, place_ref, got_ref, tiles_ref, diagonal_ref):
    hc = per - 1
    cols, height = tiles_ref.shape
    total = add_up(got_ref, per)
    top = total[:hc]
    flat = jnp.concatenate([top, pltpu.roll(top, height, 1)], axis=0)[:, :height]
    n = place_ref[1] * cols + lax.broadcasted_iota(jnp.int32, flat.shape, 0)
    m = place_ref[0] * height + lax.broadcasted_iota(jnp.int32, flat.shape, 1)
    tiles_ref[...] = jnp.where(m == n, 0.0, flat) / scale_tiles
    diagonal_ref[...] = total[hc:per, :height] / scale_diagonal


def finish(got, place, height, cols, count):
    per = cols // 2 + 1
    return pl.pallas_call(
        functools.partial(finish_kernel, float(count), float(count) ** 0.5, per),
        out_shape=(
            jax.ShapeDtypeStruct((cols, height), jnp.float32),
            jax.ShapeDtypeStruct((1, height), jnp.float32),
        ),
        in_specs=[pl.BlockSpec(memory_space=pltpu.SMEM), pl.BlockSpec(memory_space=pltpu.VMEM)],
        out_specs=[pl.BlockSpec(memory_space=pltpu.VMEM)] * 2,
        name="finish",
    )(place, pltpu.with_memory_space_constraint(got, pltpu.VMEM))


def turn(rows, axes):
    rows = rows.reshape(rows.shape[0], 1, rows.shape[1])
    rows = lax.all_to_all(rows, axes, 0, 0, tiled=True)
    return rows.reshape(rows.shape[0], rows.shape[2])


def local(three_center, coefficients, col_tiles, tile_count):
    nq, _, height, width = three_center.shape
    nz, nxl, ncore = (lax.axis_size(a) for a in AUX)
    nrow = lax.axis_size("y") * lax.axis_size("xh")
    naux = nz * nxl * ncore
    norb = coefficients.shape[0]
    rows = nrow * height
    cols = rows // naux
    core = lax.axis_index("c")

    picks = pick(coefficients, col_tiles.reshape(-1), tile_count, nrow * nxl, height)
    integrals = three_center.reshape(nq, height, width)
    picks = lax.all_to_all(picks, ("xl",) + ROW, 0, 0, tiled=True)
    chunks = [picks[n * nrow : (n + 1) * nrow] for n in range(nxl)]
    integrals, chunks = lax.optimization_barrier((integrals, chunks))
    own = lax.all_to_all(integrals, ROW, 0, 0, tiled=True)
    arrived, own = ring(chunks, "z", nz, own, nz // 2 - 1)
    blocks = chunks + arrived
    own = own.reshape(nrow, nq // nrow, height, width)
    other = lax.ppermute(own, "c", [(0, 1), (1, 0)])

    keep, send = exchange(core.reshape(1), own, other, blocks, len(blocks) - nxl, (nz, nxl, ncore))
    mine = keep + lax.ppermute(send, "c", [(0, 1), (1, 0)])
    got = summed(turn(mine, ("xl",) + ROW), nrow * nxl)
    got = turn(got, "z")

    row = lax.axis_index(ROW)
    place = jnp.stack([row, lax.axis_index(AUX)]).astype(jnp.int32)
    tiles, diagonal = finish(got, place, height, cols, nq * naux * norb * naux)
    return tiles.T, diagonal.reshape(height)


def solution(mesh):
    fine = Mesh(mesh.devices.reshape(8, 2, 2, 4, 2), AUX + ROW)
    in_specs = (P(AUX, ROW, None, None), P(AUX, None), P(ROW, None), P(ROW))
    out_specs = (P(ROW, AUX), P(ROW))
    return jax.shard_map(local, mesh=fine, in_specs=in_specs, out_specs=out_specs, check_vma=False)
```

```python
import functools

import jax
import jax.numpy as jnp
from jax import lax
from jax.experimental import pallas as pl
from jax.experimental.pallas import tpu as pltpu
from jax.sharding import Mesh, PartitionSpec as P

ROW = ("y", "xh")
AUX = ("z", "xl", "c")
A_PASS = 8
UNROLL = 8


def pick_kernel(copies, width, col_ref, count_ref, coef_ref, out_ref):
    slots = col_ref.shape[0]
    for pair in range(slots // 2):
        halves = []
        for s in (2 * pair, 2 * pair + 1):
            tile = col_ref[s]
            start = pl.multiple_of((tile // 2) * (2 * width), 2 * width)
            both = coef_ref[:, pl.ds(start, 2 * width)].astype(jnp.float32)
            want = s % 2
            swapped = pltpu.roll(both, width, 1)
            keep = jnp.full(both.shape, tile % 2, jnp.int32) == want
            live = jnp.full(both.shape, s, jnp.int32) < count_ref[0]
            halves.append(jnp.where(live, jnp.where(keep, both, swapped), 0.0))
        lane = lax.broadcasted_iota(jnp.int32, halves[0].shape, 1)
        merged = jnp.where(lane < width, halves[0], halves[1]).astype(out_ref.dtype)
        for n in range(copies):
            out_ref[n, :, pair * 2 * width : (pair + 1) * 2 * width] = merged


def pick(coefficients, cols, count, copies, width):
    norb = coefficients.shape[0]
    slots = cols.shape[0]
    return pl.pallas_call(
        functools.partial(pick_kernel, copies, width),
        out_shape=pltpu.VMEM((copies, norb, slots * width), coefficients.dtype),
        in_specs=[
            pl.BlockSpec(memory_space=pltpu.SMEM),
            pl.BlockSpec(memory_space=pltpu.SMEM),
            pl.BlockSpec(memory_space=pltpu.VMEM),
        ],
        out_specs=pl.BlockSpec(memory_space=pltpu.VMEM),
        name="pick",
    )(cols, count, coefficients)


def half_rows(part, pieces, base, half, tiles):
    _, nq, height, width = part.shape
    orbitals = sum(piece.shape[0] * piece.shape[2] for piece in pieces)

    def tile(t, _):
        start = pl.multiple_of(t * height, height)
        picked = [piece[:, t].reshape(-1, width) for piece in pieces]
        result = lax.dot_general(
            part[t].reshape(nq * height, width),
            picked[0] if len(picked) == 1 else jnp.concatenate(picked, axis=0),
            (((1,), (1,)), ((), ())),
            preferred_element_type=jnp.float32,
        ).astype(jnp.bfloat16)
        for q in range(nq):
            col = base + q * orbitals
            half[pl.ds(start, height), col : col + orbitals] = result[q * height : (q + 1) * height]
        return 0

    lax.fori_loop(tiles[0], tiles[1], tile, 0, unroll=UNROLL)
    return base + nq * orbitals


def copies_of(blocks, held, sem):
    copies = [pltpu.make_async_copy(ref, held.at[n], sem.at[n]) for n, ref in enumerate(blocks)]
    for copy in copies:
        copy.start()
    return copies


def lower_products(half, add):
    step = half.shape[0] // 2
    for i, j in ((0, 0), (1, 1), (1, 0)):
        rows, cols = slice(i * step, (i + 1) * step), slice(j * step, (j + 1) * step)
        add(
            rows,
            cols,
            lax.dot_general(
                half[rows, :], half[cols, :], (((1,), (1,)), ((), ())), preferred_element_type=jnp.float32
            ),
        )


def early_kernel(own_ref, *refs):
    *blocks, total_ref, held, sem, half = refs
    copies = copies_of(blocks, held, sem)
    base = 0
    for low in range(0, len(blocks), A_PASS):
        high = min(low + A_PASS, len(blocks))
        for copy in copies[low:high]:
            copy.wait()
        base = half_rows(own_ref, [held.at[low:high]], base, half, (0, own_ref.shape[0]))

    def add(rows, cols, block):
        total_ref[rows, cols] = block

    lower_products(half, add)


def late_kernel(nz, nxl, ncore, core_ref, own_ref, early_ref, held, other_ref, *refs):
    *blocks, keep_ref, send_ref, other, other_sem, last, sem, half, total = refs
    rows = total.shape[0]
    ntiles, nq, height, _ = own_ref.shape
    copies = copies_of(blocks, last, sem)
    parts = [pltpu.make_async_copy(other_ref.at[t], other.at[t], other_sem.at[t]) for t in range(ntiles)]
    for copy in parts:
        copy.start()
    for copy in copies:
        copy.wait()
    base = half_rows(own_ref, [last], 0, half, (0, ntiles))
    for low in range(0, ntiles, UNROLL):
        tiles = (low, low + UNROLL)
        for copy in parts[low : low + UNROLL]:
            copy.wait()
        middle = half_rows(other, [held.at[:A_PASS]], base, half, tiles)
        half_rows(other, [held.at[A_PASS : held.shape[0]], last], middle, half, tiles)

    def add(rows, cols, block):
        block = block + early_ref[rows, cols]
        total[rows, cols] = block
        if rows != cols:
            total[cols, rows] = block.T

    lower_products(half, add)
    whole = total[...]
    on_diagonal = lax.broadcasted_iota(jnp.int32, whole.shape, 0) == lax.broadcasted_iota(
        jnp.int32, whole.shape, 1
    )
    diagonal = jnp.sum(jnp.where(on_diagonal, whole, 0.0), axis=0, keepdims=True)
    cols = rows // (nz * nxl * ncore)
    nrow = rows // height
    hc = cols // 2
    low = lax.broadcasted_iota(jnp.int32, (hc, 2 * height), 1) < height
    low1 = lax.broadcasted_iota(jnp.int32, (1, 2 * height), 1) < height
    per = hc + 1
    for which, out_ref in ((0, keep_ref), (1, send_ref)):
        core = core_ref[0] if which == 0 else 1 - core_ref[0]
        for z in range(nz):
            for x in range(nxl):
                first = pl.multiple_of(((z * nxl + x) * ncore + core) * cols, cols)
                for pair in range(nrow // 2):
                    lanes = slice(pair * 2 * height, (pair + 1) * 2 * height)
                    top = total[pl.ds(first, hc), lanes]
                    bottom = total[pl.ds(pl.multiple_of(first + hc, hc), hc), lanes]
                    d = diagonal[:, lanes]
                    even = jnp.where(low, top, pltpu.roll(bottom, height, 1))
                    odd = jnp.where(low, pltpu.roll(top, height, 1), bottom)
                    base = ((x * nrow + 2 * pair) * nz + z) * per
                    out_ref[base : base + hc, :] = even
                    out_ref[base + hc : base + per, :] = jnp.where(low1, d, 0.0)
                    base += nz * per
                    out_ref[base : base + hc, :] = odd
                    out_ref[base + hc : base + per, :] = jnp.where(low1, pltpu.roll(d, height, 1), 0.0)


def exchange(core, own, other, blocks, rest, sizes):
    ntiles, nq, height, width = own.shape
    norb = blocks[0].shape[1]
    rows = ntiles * height
    nz, nxl, ncore = sizes
    cols = rows // (nz * nxl * ncore)
    messages = nz * nxl * ntiles
    count = len(blocks)
    whole = pl.BlockSpec(memory_space=pltpu.VMEM)
    blocks = [pltpu.with_memory_space_constraint(b, pltpu.HBM) for b in blocks[:rest]] + blocks[rest:]
    other = pltpu.with_memory_space_constraint(other, pltpu.HBM)
    own = pltpu.with_memory_space_constraint(own, pltpu.VMEM)

    def anywhere(n):
        return [pl.BlockSpec(memory_space=pl.ANY)] * n

    def settings(terms):
        return dict(
            compiler_params=pltpu.CompilerParams(vmem_limit_bytes=32 * 1024 * 1024),
            cost_estimate=pl.CostEstimate(
                flops=2 * nq * rows * terms * norb * (width + rows), bytes_accessed=1 << 20, transcendentals=0
            ),
        )

    total, held = pl.pallas_call(
        early_kernel,
        out_shape=(
            jax.ShapeDtypeStruct((rows, rows), jnp.float32),
            jax.ShapeDtypeStruct((rest, ntiles, norb, width), jnp.bfloat16),
        ),
        in_specs=[whole] + anywhere(rest),
        out_specs=[whole] * 2,
        scratch_shapes=[
            pltpu.SemaphoreType.DMA((rest,)),
            pltpu.VMEM((rows, nq * rest * norb), jnp.bfloat16),
        ],
        name="early",
        **settings(rest),
    )(own, *blocks[:rest])
    total = pltpu.with_memory_space_constraint(total, pltpu.VMEM)
    held = pltpu.with_memory_space_constraint(held, pltpu.VMEM)
    shape = jax.ShapeDtypeStruct((messages * (cols // 2 + 1), 2 * height), jnp.float32)
    terms = 2 * count - rest
    return pl.pallas_call(
        functools.partial(late_kernel, *sizes),
        out_shape=(shape, shape),
        in_specs=[pl.BlockSpec(memory_space=pltpu.SMEM)] + [whole] * 3 + anywhere(1 + count - rest),
        out_specs=[whole] * 2,
        scratch_shapes=[
            pltpu.VMEM(other.shape, other.dtype),
            pltpu.SemaphoreType.DMA((ntiles,)),
            pltpu.VMEM((count - rest, ntiles, norb, width), jnp.bfloat16),
            pltpu.SemaphoreType.DMA((count - rest,)),
            pltpu.VMEM((rows, nq * terms * norb), jnp.bfloat16),
            pltpu.VMEM((rows, rows), jnp.float32),
        ],
        name="late",
        **settings(terms),
    )(core, own, total, held, other, *blocks[rest:])


def ring(chunks, axis, size, beside, when):
    up = [(i, (i + 1) % size) for i in range(size)]
    down = [(i, (i - 1) % size) for i in range(size)]
    rights, lefts, got = list(chunks), list(chunks), []
    for step in range(1, size // 2 + 1):
        last = step == size // 2
        if step == when:
            rights, lefts, beside = lax.optimization_barrier((rights, lefts, beside))
        for n in range(len(chunks)):
            if not last or n % 2 == 0:
                rights[n] = lax.ppermute(rights[n], axis, up)
                got.append(rights[n])
            if not last or n % 2 == 1:
                lefts[n] = lax.ppermute(lefts[n], axis, down)
                got.append(lefts[n])
    return got, beside


def add_up(got_ref, per):
    total = got_ref[0:per, :]
    for n in range(1, got_ref.shape[0] // per):
        total = total + got_ref[n * per : (n + 1) * per, :]
    return total


def sum_kernel(got_ref, out_ref):
    out_ref[...] = add_up(got_ref, out_ref.shape[0])


def summed(got, parts):
    return pl.pallas_call(
        sum_kernel,
        out_shape=jax.ShapeDtypeStruct((got.shape[0] // parts, got.shape[1]), got.dtype),
        in_specs=[pl.BlockSpec(memory_space=pltpu.VMEM)],
        out_specs=pl.BlockSpec(memory_space=pltpu.VMEM),
        name="summed",
    )(pltpu.with_memory_space_constraint(got, pltpu.VMEM))


def finish_kernel(scale_diagonal, scale_tiles, per, place_ref, got_ref, tiles_ref, diagonal_ref):
    hc = per - 1
    cols, height = tiles_ref.shape
    total = add_up(got_ref, per)
    top = total[:hc]
    flat = jnp.concatenate([top, pltpu.roll(top, height, 1)], axis=0)[:, :height]
    n = place_ref[1] * cols + lax.broadcasted_iota(jnp.int32, flat.shape, 0)
    m = place_ref[0] * height + lax.broadcasted_iota(jnp.int32, flat.shape, 1)
    tiles_ref[...] = jnp.where(m == n, 0.0, flat) / scale_tiles
    diagonal_ref[...] = total[hc:per, :height] / scale_diagonal


def finish(got, place, height, cols, count):
    per = cols // 2 + 1
    return pl.pallas_call(
        functools.partial(finish_kernel, float(count), float(count) ** 0.5, per),
        out_shape=(
            jax.ShapeDtypeStruct((cols, height), jnp.float32),
            jax.ShapeDtypeStruct((1, height), jnp.float32),
        ),
        in_specs=[pl.BlockSpec(memory_space=pltpu.SMEM), pl.BlockSpec(memory_space=pltpu.VMEM)],
        out_specs=[pl.BlockSpec(memory_space=pltpu.VMEM)] * 2,
        name="finish",
    )(place, pltpu.with_memory_space_constraint(got, pltpu.VMEM))


def turn(rows, axes):
    rows = rows.reshape(rows.shape[0], 1, rows.shape[1])
    rows = lax.all_to_all(rows, axes, 0, 0, tiled=True)
    return rows.reshape(rows.shape[0], rows.shape[2])


def local(three_center, coefficients, col_tiles, tile_count):
    nq, _, height, width = three_center.shape
    nz, nxl, ncore = (lax.axis_size(a) for a in AUX)
    nrow = lax.axis_size("y") * lax.axis_size("xh")
    naux = nz * nxl * ncore
    norb = coefficients.shape[0]
    rows = nrow * height
    cols = rows // naux
    core = lax.axis_index("c")

    picks = pick(coefficients, col_tiles.reshape(-1), tile_count, nrow * nxl, height)
    integrals = three_center.reshape(nq, height, width)
    picks = lax.all_to_all(picks, ("xl",) + ROW, 0, 0, tiled=True)
    chunks = [picks[n * nrow : (n + 1) * nrow] for n in range(nxl)]
    integrals, chunks = lax.optimization_barrier((integrals, chunks))
    own = lax.all_to_all(integrals, ROW, 0, 0, tiled=True)
    arrived, own = ring(chunks, "z", nz, own, 4)
    blocks = chunks + arrived
    own = own.reshape(nrow, nq // nrow, height, width)
    other = lax.ppermute(own, "c", [(0, 1), (1, 0)])

    keep, send = exchange(core.reshape(1), own, other, blocks, len(blocks) - nxl, (nz, nxl, ncore))
    mine = keep + lax.ppermute(send, "c", [(0, 1), (1, 0)])
    got = summed(turn(mine, ("xl",) + ROW), nrow * nxl)
    got = turn(got, "z")

    row = lax.axis_index(ROW)
    place = jnp.stack([row, lax.axis_index(AUX)]).astype(jnp.int32)
    tiles, diagonal = finish(got, place, height, cols, nq * naux * norb * naux)
    return tiles.T, diagonal.reshape(height)


def solution(mesh):
    fine = Mesh(mesh.devices.reshape(8, 2, 2, 4, 2), AUX + ROW)
    in_specs = (P(AUX, ROW, None, None), P(AUX, None), P(ROW, None), P(ROW))
    out_specs = (P(ROW, AUX), P(ROW))
    return jax.shard_map(local, mesh=fine, in_specs=in_specs, out_specs=out_specs, check_vma=False)
```
